32 devices in a mesh: groups: 2 (over y), tok: 4 (over z), width: 2 (over x), sub: 2 (over core).
Axes of the slice: x: 2, y: 2, z: 4, core: 2. Of those that a mesh axis runs over, the one named last changes fastest.
Arguments:
- activation: float32 [3072, 8192], P(('groups', 'tok', 'sub'), 'width'), parts along dimension 0, may hold values from -6 to 6
- cotangent: float32 [3072, 8192], P(('groups', 'tok', 'sub'), 'width'), parts along dimension 0, may hold values from -6 to 6
- query_output_factor: bfloat16 [32, 32, 8192], P(('groups', 'tok'), 'sub', 'width'), parts along dimension 0, may hold values from -0.0625 to 0.0625
- query_input_factor: bfloat16 [32, 32, 8192], P(('groups', 'tok'), 'sub', 'width'), parts along dimension 0, may hold values from -0.01171875 to 0.01171875
- query_dest: int32 [32, 1], P(('groups', 'tok')), parts along dimension 0, may hold values from 0 to 3; in each aligned block of 4 rows (0 to 3, 4 to 7, ...) at most 2 rows name the same one
- query_cluster: int32 [32, 1], P(('groups', 'tok')), parts along dimension 0, may hold values from 0 to 1
- token_cluster: int32 [3072], P(('groups', 'tok')), parts along dimension 0, may hold values from 0 to 1
- token_count: int32 [16], P('groups'), parts along dimension 0, may hold values from 1 to 192, 1152 in all
Outputs:
- scores: float32 [3072, 16], P(('groups', 'tok', 'width', 'sub')), parts along dimension 0
The draws below stay inside these ranges and needn't reach their ends.
There are 2 independent parts, one for each index of `groups`. The reference program is written for one: setup_inputs(seed, part) draws one part's arguments, and reference() takes and returns one part's arrays. A program takes and returns all parts, laid end to end along the dimension named above; each array names one. Nothing has to cross between parts.
Inputs may be any that keep to these rules, and one draw needn't show every extreme that they name: `query_dest`: each row names 1 tok index; among the 4 queries of one tok index no tok index is named more than 2 times, a bound that some block reaches. `token_count`: the live slots are the first ones of a device; some device has all 192 live.
All inputs are finite; a program needn't handle non-finite values.
Results may differ from the reference program's by a relative error of at most 0.0003.
Values may be sent and summed in bfloat16 or wider, within the bound.
A program may use at most 64 MiB of HBM per device.

```python
import math
import jax
import jax.numpy as jnp
import numpy as np
from jax import lax

D = 8192
RANK = 32
TOK_DEV = 192
Q_DEV = 4
CAP = 2
CL_DEV = 2
TOPC = 1
BLOCK_ROWS = 384
TOKENS = 1536
QUERIES = 16
N_TOK = 4
N_SUB = 2


def place_ends(values, stream_key, low, high):
    place = [jax.random.randint(jax.random.fold_in(stream_key, axis), (), 0, length) for axis, length in enumerate(values.shape)]
    widest = values.shape.index(max(values.shape))
    neighbour = place[:widest] + [(place[widest] + 1) % values.shape[widest]] + place[widest + 1:]
    return values.at[tuple(place)].set(low).at[tuple(neighbour)].set(high)


def shard_levels(stream_key, dims, shards, low, top_value):
    gain = 1.0
    for position, blocks in shards:
        heights = jax.random.uniform(jax.random.fold_in(jax.random.fold_in(stream_key, 6), position), (blocks,), jnp.float32, low / len(shards), top_value / len(shards))
        gain = gain * jnp.repeat(jnp.exp(heights), dims[position] // blocks).reshape((-1,) + (1,) * (len(dims) - 1 - position))
    return gain


def profile(amount, total, most, skew):
    loads = [(1 << 20) // math.isqrt(grade ** skew) + 1 for grade in range(2, amount + 1)]
    surplus, counts = total - most - (amount - 1), [1] * (amount - 1)
    while surplus > 0:
        movable = [i for i in range(amount - 1) if counts[i] < most]
        pool, budget = sum([loads[i] for i in movable]), surplus
        for i in movable:
            addition = min(most - counts[i], max(1, budget * loads[i] // pool), surplus)
            counts[i] = counts[i] + addition
            surplus = surplus - addition
    return np.array([most] + counts)


def uneven_parts(own_key, amount, total, limit, lean):
    if amount == 2:
        one = jax.random.randint(own_key, (), max(1, total - limit), min(limit, total - 1) + 1)
        return jnp.stack([one, total - one])
    lengths = jnp.asarray(profile(amount, total, limit, lean), jnp.int32)
    twos = (amount - 1) // 2
    donor, sink = lengths[1:1 + 2 * twos:2], lengths[2:2 + 2 * twos:2]
    room = jnp.minimum(donor - 1, limit - sink)
    shifted = jax.random.randint(jax.random.fold_in(own_key, 1), (twos,), 0, 1 << 20) % (room + 1)
    lengths = lengths.at[1:1 + 2 * twos:2].set(donor - shifted).at[2:2 + 2 * twos:2].set(sink + shifted)
    return lengths[jax.random.permutation(jax.random.fold_in(own_key, 2), amount)]


def deal_out(stream_key, own, number, rows, count, top, reach, slope):
    order = jax.random.permutation(stream_key, count)
    packed, ordinary = shares(count, rows * top, reach, slope, True), shares(count, rows * top, reach, slope, False)
    places = jnp.arange(count)

    def named(lengths, offset_by):
        used = int((lengths > 0).sum())
        fixed = max(1, used // 4)
        moved = fixed + (places - fixed + offset_by * (used - fixed)) % max(1, count - fixed)
        return jnp.zeros((count,), jnp.int32).at[order[jnp.where(places < fixed, places, moved)]].set(jnp.asarray(lengths, jnp.int32))

    lengths = jnp.where(number % 4 == 0, named(packed, number // 4), named(ordinary, number - number // 4 - 1))
    mixed = jax.random.permutation(jax.random.fold_in(own, 3), count)
    giver, taker = mixed[0:count // 2 * 2:2], mixed[1:count // 2 * 2:2]
    slack = jnp.minimum(lengths[giver] - 1, reach - lengths[taker]) // 2
    slack = jnp.where((giver == order[0]) | (taker == order[0]) | (lengths[taker] == 0), 0, jnp.maximum(slack, 0))
    moved = jax.random.randint(jax.random.fold_in(own, 4), (count // 2,), 0, 1 << 20) % (slack + 1)
    lengths = lengths.at[giver].add(-moved).at[taker].add(moved)
    labels = jnp.searchsorted(jnp.cumsum(lengths), jnp.arange(rows * top), side="right").astype(jnp.int32)
    listing = labels.reshape(top, rows).T
    listing = listing[jax.random.permutation(jax.random.fold_in(own, 1), rows)]
    offset_by = jax.random.randint(jax.random.fold_in(own, 2), (rows, 1), 0, top)
    return jnp.take_along_axis(listing, (jnp.arange(top)[None, :] + offset_by) % top, axis=1)


def shares(count, total, bound, lean, full):
    portions = [(1 << 20) // math.isqrt(rank ** lean) + 1 for rank in range(1, count + 1)]
    largest = bound if full else min(bound, max(-(-total // count), total * portions[0] // sum(portions)))
    least = 1 if total - largest >= count - 1 else 0
    given, spare = [largest] + [least] * (count - 1), total - largest - least * (count - 1)
    while spare > 0:
        candidates = [i for i in range(1, count) if given[i] < largest] or [i for i in range(1, count) if given[i] < bound]
        mass, budget = sum([portions[i] for i in candidates]), spare
        for i in candidates:
            more = min(bound - given[i], max(1, budget * portions[i] // mass), spare)
            given[i] = given[i] + more
            spare = spare - more
    return np.array(given)


def normal_values(stream_key, shape, width, limit, cuts=(), held_as=jnp.bfloat16):
    entries = jax.random.normal(stream_key, shape, jnp.float32) * width
    if len(cuts) > 0:
        entries = shard_levels(stream_key, shape, cuts, -0.22, 0.18) * entries
    return jnp.clip(entries, min=-limit, max=limit).astype(held_as)


def setup_inputs(seed: int = 0, part: int = 0) -> dict:
    key_list = jax.random.split(jax.random.key(seed), 9)
    own_keys = jax.random.split(jax.random.fold_in(key_list[8], part), 9)
    activation = normal_values(own_keys[0], (TOKENS, D), 1.0, 6.0, ((0, 8), (1, 2)), jnp.float32)
    cotangent = normal_values(own_keys[1], (TOKENS, D), 1.0, 6.0, ((0, 8), (1, 2)), jnp.float32)
    query_output_factor = normal_values(own_keys[2], (QUERIES, RANK, D), D ** -0.5, 0.0625, ((0, 4), (1, 2), (2, 2)))
    query_input_factor = normal_values(own_keys[3], (QUERIES, RANK, D), (D * RANK) ** -0.5, 0.01171875, ((0, 4), (1, 2), (2, 2)))
    query_dest_keys = jax.random.split(jax.random.fold_in(own_keys[4], 1), QUERIES // Q_DEV)
    query_dest_turns = jax.random.permutation(jax.random.fold_in(own_keys[4], 3), QUERIES // Q_DEV)
    query_dest = jax.vmap(lambda own, number: deal_out(jax.random.fold_in(own_keys[4], 2), own, number, Q_DEV, N_TOK, TOPC, CAP, 2))(query_dest_keys, query_dest_turns).reshape((QUERIES, TOPC))
    query_cluster = place_ends(jax.random.randint(own_keys[5], (QUERIES, TOPC), 0, CL_DEV), jax.random.fold_in(own_keys[5], 1), 0, CL_DEV - 1).astype(jnp.int32)
    token_cluster = place_ends(jax.random.randint(own_keys[6], (TOKENS,), 0, CL_DEV), jax.random.fold_in(own_keys[6], 1), 0, CL_DEV - 1).astype(jnp.int32)
    token_count = uneven_parts(own_keys[7], N_TOK * N_SUB, 3 * TOK_DEV * N_TOK * N_SUB // 4, TOK_DEV, 2).astype(jnp.int32)
    return dict(activation=activation, cotangent=cotangent, query_output_factor=query_output_factor, query_input_factor=query_input_factor, query_dest=query_dest, query_cluster=query_cluster, token_cluster=token_cluster, token_count=token_count)


def reference(activation, cotangent, query_output_factor, query_input_factor, query_dest, query_cluster, token_cluster, token_count):
    rows = jnp.arange(TOKENS, dtype=jnp.int32)
    valid = (rows % TOK_DEV) < token_count[rows // TOK_DEV]
    block = rows // BLOCK_ROWS
    hits = (query_dest[None, :, :] == block[:, None, None]) & (query_cluster[None, :, :] == token_cluster[:, None, None])
    live = (jnp.any(hits, axis=-1) & valid[:, None]).astype(jnp.float32)
    u_blocks = query_output_factor.reshape(N_TOK, Q_DEV, RANK, D)
    v_blocks = query_input_factor.reshape(N_TOK, Q_DEV, RANK, D)

    def one_block(pair):
        u_part, v_part = pair
        u_flat = u_part.astype(jnp.float32).reshape(Q_DEV * RANK, D)
        v_flat = v_part.astype(jnp.float32).reshape(Q_DEV * RANK, D)
        grad_proj = jnp.dot(cotangent, u_flat.T, precision=lax.Precision.HIGHEST, preferred_element_type=jnp.float32)
        act_proj = jnp.dot(activation, v_flat.T, precision=lax.Precision.HIGHEST, preferred_element_type=jnp.float32)
        return jnp.sum((grad_proj * act_proj).reshape(TOKENS, Q_DEV, RANK), axis=-1)

    stacked = lax.map(one_block, (u_blocks, v_blocks))
    full = jnp.transpose(stacked, (1, 0, 2)).reshape(TOKENS, QUERIES)
    return live * full
```

```python
import functools

import jax
import jax.numpy as jnp
from jax import lax
from jax.experimental import pallas as pl
from jax.experimental.pallas import tpu as pltpu
from jax.sharding import PartitionSpec as P

CAP = 2
MESH = pl.DeviceIdType.MESH


def kernel(
    ntok,
    nwide,
    nsub,
    chunks,
    act_hbm,
    cot_hbm,
    u_ref,
    v_ref,
    dest_ref,
    clus_ref,
    tc_ref,
    cnt_ref,
    out_ref,
    tokens,
    high,
    low,
    outbox,
    inbox,
    acc,
    parts,
    meta_out,
    meta_in,
    load_sem,
    tok_send,
    tok_recv,
    meta_send,
    meta_recv,
    fac_send,
    fac_recv,
    part_send,
    part_recv,
):
    mine = lax.axis_index("tok")
    column = lax.axis_index("width")
    half = lax.axis_index("sub")
    local_q, topc = dest_ref.shape
    rows_dev, depth = act_hbm.shape
    block_rows = rows_dev * nsub
    rank = u_ref.shape[1]
    lanes = meta_out.shape[1]
    piece = depth // chunks
    nquad = nwide * nsub
    quad = column * nsub + half
    share = block_rows // nquad
    sources = (cot_hbm, act_hbm)
    factors = (u_ref, v_ref)
    half_row = pl.multiple_of(half * rows_dev, 8)

    def quad_device(offset):
        place = lax.rem(quad + offset, nquad)
        return place, {"width": lax.div(place, nsub), "sub": lax.rem(place, nsub)}

    barrier = pltpu.get_barrier_semaphore()
    for j in range(1, ntok):
        pl.semaphore_signal(
            barrier, inc=1, device_id={"tok": lax.rem(mine + j, ntok)}, device_id_type=MESH
        )
    for i in range(1, nquad):
        pl.semaphore_signal(barrier, inc=1, device_id=quad_device(i)[1], device_id_type=MESH)

    loads = [
        pltpu.make_async_copy(
            sources[f], tokens.at[f, pl.ds(half_row, rows_dev), :], load_sem.at[f]
        )
        for f in range(2)
    ]
    for load in loads:
        load.start()

    line = lax.broadcasted_iota(jnp.int32, meta_out.shape, 0)
    lane = lax.broadcasted_iota(jnp.int32, meta_out.shape, 1)
    meta = jnp.zeros(meta_out.shape, jnp.int32)
    for a in range(local_q):
        here = lane == mine * local_q + a
        for k in range(topc):
            meta = jnp.where(here & (line == k), dest_ref[a, k], meta)
            meta = jnp.where(here & (line == topc + k), clus_ref[a, k], meta)
    meta_out[...] = meta
    meta_in[0] = meta

    def picked(target):
        seen = jnp.int32(0)
        found = [jnp.int32(0) for _ in range(CAP)]
        for a in range(local_q):
            named = dest_ref[a, 0] == target
            for k in range(1, topc):
                named = jnp.logical_or(named, dest_ref[a, k] == target)
            for e in range(CAP):
                found[e] = jnp.where(jnp.logical_and(named, seen == e), a, found[e])
            seen = seen + named.astype(jnp.int32)
        return found

    def pack(f):
        def one(j, carry):
            found = picked(lax.rem(mine + j, ntok))
            for e in range(CAP):
                outbox[f, j, e * rank : (e + 1) * rank, :] = factors[f][found[e]]
            return carry

        lax.fori_loop(1, ntok, one, 0)
        found = picked(mine)
        for e in range(CAP):
            inbox[f, 0, e * rank : (e + 1) * rank, :] = factors[f][found[e]]

    def fac_copy(f, c, j):
        cols = pl.ds(c * piece, piece)
        return pltpu.make_async_remote_copy(
            src_ref=outbox.at[f, j, :, cols],
            dst_ref=inbox.at[f, j, :, cols],
            send_sem=fac_send.at[f, c],
            recv_sem=fac_recv.at[f, c],
            device_id={"tok": lax.rem(mine + j, ntok)},
            device_id_type=MESH,
        )

    def fac_start(f, c):
        def one(j, carry):
            fac_copy(f, c, j).start()
            return carry

        lax.fori_loop(1, ntok, one, 0)

    def fac_all(f, c):
        cols = pl.ds(c * piece, piece)
        return pltpu.make_async_remote_copy(
            src_ref=outbox.at[f, pl.ds(1, ntok - 1), :, cols],
            dst_ref=inbox.at[f, pl.ds(1, ntok - 1), :, cols],
            send_sem=fac_send.at[f, c],
            recv_sem=fac_recv.at[f, c],
            device_id={"tok": lax.rem(mine + 1, ntok)},
            device_id_type=MESH,
        )

    def meta_copy(j):
        return pltpu.make_async_remote_copy(
            src_ref=meta_out,
            dst_ref=meta_in.at[j],
            send_sem=meta_send.at[j],
            recv_sem=meta_recv.at[j],
            device_id={"tok": lax.rem(mine + j, ntok)},
            device_id_type=MESH,
        )

    def tok_copy(f, i):
        return pltpu.make_async_remote_copy(
            src_ref=sources[f],
            dst_ref=tokens.at[f, pl.ds(half_row, rows_dev), :],
            send_sem=tok_send.at[f, i],
            recv_sem=tok_recv.at[f, i],
            device_id={"sub": lax.rem(half + i, nsub)},
            device_id_type=MESH,
        )

    def part_copy(f, i):
        place, device = quad_device(i)
        return pltpu.make_async_remote_copy(
            src_ref=acc.at[f, pl.ds(pl.multiple_of(place * share, 8), share), :],
            dst_ref=parts.at[f, i],
            send_sem=part_send.at[f, i],
            recv_sem=part_recv.at[f, i],
            device_id=device,
            device_id_type=MESH,
        )

    pack(0)
    pl.semaphore_wait(barrier, ntok - 1 + nquad - 1)
    for c in range(chunks):
        fac_start(0, c)
    for i in range(1, nsub):
        tok_copy(0, i).start()

    def meta_go(j, carry):
        meta_copy(j).start()
        return carry

    lax.fori_loop(1, ntok, meta_go, 0)
    for i in range(1, nsub):
        tok_copy(1, i).start()
    pack(1)

    step = 16

    def split(f, base):
        @pl.loop(0, rows_dev // step)
        def _(b):
            rows = pl.ds(pl.multiple_of(base + b * step, step), step)
            value = tokens[f, rows, :]
            top = value.astype(jnp.bfloat16)
            high[f, rows, :] = top
            low[f, rows, :] = (value - top.astype(jnp.float32)).astype(jnp.bfloat16)

    tile = 128

    def multiply(f, c):
        cols = pl.ds(c * piece, piece)

        @pl.loop(0, block_rows // tile)
        def _(b):
            rows = pl.ds(pl.multiple_of(b * tile, tile), tile)
            weight = inbox[f, :, :, cols].reshape(ntok * CAP * rank, piece)
            dims = (((1,), (1,)), ((), ()))
            value = lax.dot_general(
                high[f, rows, cols], weight, dims, preferred_element_type=jnp.float32
            ) + lax.dot_general(
                low[f, rows, cols], weight, dims, preferred_element_type=jnp.float32
            )
            if c == 0:
                acc[f, rows, :] = value
            else:
                acc[f, rows, :] += value

    for f in range(2):
        loads[f].wait()
        split(f, half * rows_dev)

    def meta_wait(j, carry):
        meta_copy(j).wait()
        return carry

    lax.fori_loop(1, ntok, meta_wait, 0)
    lists = jnp.sum(meta_in[...], axis=0)
    lane1 = lax.broadcasted_iota(jnp.int32, (8, lanes), 1)
    arrived = jnp.zeros((8, lanes), jnp.int32)
    label = jnp.zeros((8, lanes), jnp.int32)
    for k in range(topc):
        hit = (jnp.broadcast_to(lists[k : k + 1], (8, lanes)) == mine) & (lane1 < ntok * local_q)
        arrived = jnp.where(hit, 1, arrived)
        label = jnp.where(hit, jnp.broadcast_to(lists[topc + k : topc + k + 1], (8, lanes)), label)
    slot = jnp.zeros((8, lanes), jnp.int32)
    for a in range(1, local_q):
        slot = slot + jnp.where(
            lax.rem(lane1, local_q) >= a, pltpu.roll(arrived, a, axis=1), 0
        )
    width = ntok * CAP * rank
    place = lax.broadcasted_iota(jnp.int32, (width, lanes), 0)
    query = lax.broadcasted_iota(jnp.int32, (width, lanes), 1)
    origin = lax.rem(mine - lax.div(place, CAP * rank) + ntok, ntok)
    seat = lax.rem(lax.div(place, rank), CAP)
    chosen = (
        (arrived[0:1] == 1) & (slot[0:1] == seat) & (lax.div(query, local_q) == origin)
    )
    mapping = chosen.astype(jnp.float32)
    base = quad * share
    wide = tc_ref.shape[1]
    row = lax.broadcasted_iota(jnp.int32, (share, wide), 0) + base
    other = lax.broadcasted_iota(jnp.int32, (share, wide), 1)
    row_cluster = jnp.sum(
        jnp.where(row == other, tc_ref[...], 0).astype(jnp.float32), axis=1, keepdims=True
    )
    spot = lax.broadcasted_iota(jnp.int32, (share, lanes), 0) + base
    owner = lax.div(spot, rows_dev)
    limit = jnp.zeros((share, lanes), jnp.int32)
    for i in range(nsub):
        limit = jnp.where(owner == i, cnt_ref[mine * nsub + i], limit)
    live = (lax.rem(spot, rows_dev) < limit) & (row_cluster == label[0:1].astype(jnp.float32))
    live = live.astype(jnp.float32)

    for f in range(2):
        for i in range(1, nsub):
            tok_copy(f, i).wait()
            split(f, lax.rem(half + nsub - i, nsub) * rows_dev)
        for c in range(chunks):
            fac_all(f, c).wait_recv()
            if f == 0:
                fac_start(1, c)
            multiply(f, c)
        for i in range(1, nquad):
            part_copy(f, i).start()

    def total(f, h):
        start = pl.multiple_of(quad * share, 8)
        value = acc[f, pl.ds(start, share), :] if h == 0 else parts[f, h]
        for i in range(h + nsub, nquad, nsub):
            value = value + parts[f, i]
        return value

    for i in range(1, nquad):
        part_copy(0, i).wait_recv()
    for i in range(1, nquad):
        part_copy(1, i).wait_recv()
    product = total(0, 0) * total(1, 0)
    for h in range(1, nsub):
        product = product + total(0, h) * total(1, h)
    result = live * lax.dot_general(
        product,
        mapping,
        (((1,), (0,)), ((), ())),
        precision=lax.Precision.HIGHEST,
        preferred_element_type=jnp.float32,
    )
    out_ref[...] = result[:, : out_ref.shape[1]]

    for f in range(2):
        for c in range(chunks):
            fac_all(f, c).wait_send()
        for i in range(1, nquad):
            part_copy(f, i).wait_send()


def on_device(
    activation,
    cotangent,
    query_output_factor,
    query_input_factor,
    query_dest,
    query_cluster,
    token_cluster,
    token_count,
):
    ntok = lax.axis_size("tok")
    nsub = lax.axis_size("sub")
    nwide = lax.axis_size("width")
    local_q, topc = query_dest.shape
    rows_dev, depth = activation.shape
    rank = query_output_factor.shape[1]
    block_rows = rows_dev * nsub
    nquad = nwide * nsub
    share = block_rows // nquad
    lanes = -(-ntok * local_q // 128) * 128
    lines = -(-2 * topc // 8) * 8
    width = ntok * CAP * rank
    chunks = 4
    dma = pltpu.SemaphoreType.DMA
    vmem = pl.BlockSpec(memory_space=pltpu.VMEM)
    smem = pl.BlockSpec(memory_space=pltpu.SMEM)
    hbm = pl.BlockSpec(memory_space=pl.ANY)
    return pl.pallas_call(
        functools.partial(kernel, ntok, nwide, nsub, chunks),
        out_shape=jax.ShapeDtypeStruct((share, ntok * local_q), jnp.float32),
        in_specs=[hbm, hbm, vmem, vmem, smem, smem, vmem, smem],
        out_specs=vmem,
        scratch_shapes=[
            pltpu.VMEM((2, block_rows, depth), jnp.float32),
            pltpu.VMEM((2, block_rows, depth), jnp.bfloat16),
            pltpu.VMEM((2, block_rows, depth), jnp.bfloat16),
            pltpu.VMEM((2, ntok, CAP * rank, depth), jnp.bfloat16),
            pltpu.VMEM((2, ntok, CAP * rank, depth), jnp.bfloat16),
            pltpu.VMEM((2, block_rows, width), jnp.float32),
            pltpu.VMEM((2, nquad, share, width), jnp.float32),
            pltpu.VMEM((lines, lanes), jnp.int32),
            pltpu.VMEM((ntok, lines, lanes), jnp.int32),
            dma((2,)),
            dma((2, nsub)),
            dma((2, nsub)),
            dma((ntok,)),
            dma((ntok,)),
            dma((2, chunks)),
            dma((2, chunks)),
            dma((2, nquad)),
            dma((2, nquad)),
        ],
        compiler_params=pltpu.CompilerParams(
            collective_id=0, has_side_effects=True, vmem_limit_bytes=56 * 2**20
        ),
    )(
        activation,
        cotangent,
        query_output_factor,
        query_input_factor,
        query_dest,
        query_cluster,
        token_cluster.reshape(1, block_rows),
        token_count,
    )


def solution(mesh):
    placed = (
        P(("groups", "tok", "sub"), "width"),
        P(("groups", "tok", "sub"), "width"),
        P(("groups", "tok"), "sub", "width"),
        P(("groups", "tok"), "sub", "width"),
        P(("groups", "tok"), None),
        P(("groups", "tok"), None),
        P(("groups", "tok")),
        P("groups"),
    )
    return jax.shard_map(
        on_device,
        mesh=mesh,
        in_specs=placed,
        out_specs=P(("groups", "tok", "width", "sub"), None),
        check_vma=False,
    )
```

```python
import functools

import jax
import jax.numpy as jnp
from jax import lax
from jax.experimental import pallas as pl
from jax.experimental.pallas import tpu as pltpu
from jax.sharding import PartitionSpec as P

CAP = 2
MESH = pl.DeviceIdType.MESH


def over_lanes(lists, topc, local_q, count):
    shape = (8, lists.shape[1])
    lane = lax.broadcasted_iota(jnp.int32, shape, 1)
    named = [jnp.broadcast_to(lists[k : k + 1], shape) for k in range(topc)]
    total = jnp.zeros(shape, jnp.int32)
    for k in range(topc):
        again = jnp.zeros(shape, jnp.int32)
        for a in range(1, local_q):
            earlier = (lax.rem(lane, local_q) >= a) & (lane < count)
            for other in range(topc):
                same = named[k] == pltpu.roll(named[other], a, axis=1)
                again = jnp.where(earlier & same, 1, again)
        total = total + again
    return total


def meta_kernel(
    ngroup, ntok, dest_ref, clus_ref, lists_ref, count_ref, meta_out, meta_in, send, recv
):
    group = lax.axis_index("groups")
    mine = lax.axis_index("tok")
    topc, local_q = dest_ref.shape
    everyone = ngroup * ntok

    def device(p):
        return {
            "groups": lax.rem(group + lax.div(p, ntok), ngroup),
            "tok": lax.rem(mine + lax.rem(p, ntok), ntok),
        }

    barrier = pltpu.get_barrier_semaphore()

    def greet(p, carry):
        pl.semaphore_signal(barrier, inc=1, device_id=device(p), device_id_type=MESH)
        return carry

    lax.fori_loop(1, everyone, greet, 0)
    line = lax.broadcasted_iota(jnp.int32, meta_out.shape, 0)
    lane = lax.broadcasted_iota(jnp.int32, meta_out.shape, 1)
    meta = jnp.zeros(meta_out.shape, jnp.int32)
    for a in range(local_q):
        here = lane == mine * local_q + a
        for k in range(topc):
            meta = jnp.where(here & (line == k), dest_ref[k, a], meta)
            meta = jnp.where(here & (line == topc + k), clus_ref[k, a], meta)
    meta_out[...] = meta
    meta_in[0] = meta
    pl.semaphore_wait(barrier, everyone - 1)

    def copy(p):
        return pltpu.make_async_remote_copy(
            src_ref=meta_out,
            dst_ref=meta_in.at[p],
            send_sem=send.at[p],
            recv_sem=recv.at[p],
            device_id=device(p),
            device_id_type=MESH,
        )

    def go(p, carry):
        copy(p).start()
        return carry

    def done(p, carry):
        copy(p).wait()
        return carry

    lax.fori_loop(1, everyone, go, 0)
    lax.fori_loop(1, everyone, done, 0)
    most = jnp.float32(0)
    for g in range(ngroup):
        lists = jnp.sum(meta_in[g * ntok : (g + 1) * ntok], axis=0)
        if g == 0:
            lists_ref[...] = lists
        over = over_lanes(lists, topc, local_q, ntok * local_q)
        most = jnp.maximum(most, jnp.sum(over[0:1].astype(jnp.float32)))
    count_ref[0] = most.astype(jnp.int32)


def kernel(
    ntok,
    nwide,
    nsub,
    chunks,
    lean,
    act_hbm,
    cot_hbm,
    u_ref,
    v_ref,
    dest_ref,
    lists_ref,
    tc_ref,
    cnt_ref,
    out_ref,
    tokens,
    high,
    low,
    outbox,
    inbox,
    acc,
    parts,
    relay,
    load_sem,
    tok_send,
    tok_recv,
    relay_send,
    relay_recv,
    fac_send,
    fac_recv,
    part_send,
    part_recv,
):
    mine = lax.axis_index("tok")
    column = lax.axis_index("width")
    half = lax.axis_index("sub")
    topc, local_q = dest_ref.shape
    rows_dev, depth = act_hbm.shape
    block_rows = rows_dev * nsub
    rank = u_ref.shape[1]
    lanes = lists_ref.shape[1]
    seats = 1 if lean else CAP
    places = inbox.shape[1]
    piece = depth // chunks
    nquad = nwide * nsub
    quad = column * nsub + half
    share = block_rows // nquad
    sources = (cot_hbm, act_hbm)
    factors = (u_ref, v_ref)
    half_row = pl.multiple_of(half * rows_dev, 8)

    def quad_device(offset):
        place = lax.rem(quad + offset, nquad)
        return place, {"width": lax.div(place, nsub), "sub": lax.rem(place, nsub)}

    barrier = pltpu.get_barrier_semaphore()
    for j in range(1, ntok):
        pl.semaphore_signal(
            barrier, inc=1, device_id={"tok": lax.rem(mine + j, ntok)}, device_id_type=MESH
        )
    for i in range(1, nquad):
        pl.semaphore_signal(barrier, inc=1, device_id=quad_device(i)[1], device_id_type=MESH)

    loads = [
        pltpu.make_async_copy(
            sources[f], tokens.at[f, pl.ds(half_row, rows_dev), :], load_sem.at[f]
        )
        for f in range(2)
    ]
    for load in loads:
        load.start()

    def picked(target):
        seen = jnp.int32(0)
        found = [jnp.int32(0) for _ in range(CAP)]
        for a in range(local_q):
            named = dest_ref[0, a] == target
            for k in range(1, topc):
                named = jnp.logical_or(named, dest_ref[k, a] == target)
            for e in range(CAP):
                found[e] = jnp.where(jnp.logical_and(named, seen == e), a, found[e])
            seen = seen + named.astype(jnp.int32)
        return found

    extra = jnp.int32(0)
    holds = jnp.int32(0)
    for a in range(1, local_q):
        for before in range(a):
            for k in range(topc):
                for other in range(topc):
                    same = dest_ref[k, a] == dest_ref[other, before]
                    extra = jnp.where(same, a, extra)
                    holds = jnp.where(same, 1, holds)

    def relay_copy(f, c, way):
        cols = pl.ds(c * piece, piece)
        step = 1 if way == 0 else ntok - 1
        return pltpu.make_async_remote_copy(
            src_ref=relay.at[way, f, :, cols],
            dst_ref=inbox.at[f, ntok + way, :, cols],
            send_sem=relay_send.at[way, f, c],
            recv_sem=relay_recv.at[way, f, c],
            device_id={"tok": lax.rem(mine + step, ntok)},
            device_id_type=MESH,
        )

    first, last = mine == 0, mine == ntok - 1

    def forward(f, c):
        cols = pl.ds(c * piece, piece)
        for way in range(2):
            starts, ends = (first, last) if way == 0 else (last, first)

            @pl.when(jnp.logical_not(starts))
            def _():
                relay_copy(f, c, way).wait_recv()

            @pl.when(jnp.logical_not(ends))
            def _():
                relay[way, f, :, cols] = jnp.where(
                    holds == 1, inbox[f, ntok + 2, :, cols], inbox[f, ntok + way, :, cols]
                )
                relay_copy(f, c, way).start()

    def pack(f):
        def one(j, carry):
            found = picked(lax.rem(mine + j, ntok))
            for e in range(seats):
                outbox[f, j, e * rank : (e + 1) * rank, :] = factors[f][found[e]]
            return carry

        lax.fori_loop(1, ntok, one, 0)
        found = picked(mine)
        for e in range(seats):
            inbox[f, 0, e * rank : (e + 1) * rank, :] = factors[f][found[e]]
        if lean:
            value = factors[f][extra]
            inbox[f, ntok + 2] = value
            inbox[f, ntok + 3] = value

            @pl.when(mine == 0)
            def _():
                inbox[f, ntok] = jnp.zeros_like(value)

            @pl.when(mine == ntok - 1)
            def _():
                inbox[f, ntok + 1] = jnp.zeros_like(value)

    def fac_copy(f, c, j):
        cols = pl.ds(c * piece, piece)
        return pltpu.make_async_remote_copy(
            src_ref=outbox.at[f, j, :, cols],
            dst_ref=inbox.at[f, j, :, cols],
            send_sem=fac_send.at[f, c],
            recv_sem=fac_recv.at[f, c],
            device_id={"tok": lax.rem(mine + j, ntok)},
            device_id_type=MESH,
        )

    def fac_start(f, c):
        def one(j, carry):
            fac_copy(f, c, j).start()
            return carry

        lax.fori_loop(1, ntok, one, 0)

    def fac_all(f, c):
        cols = pl.ds(c * piece, piece)
        return pltpu.make_async_remote_copy(
            src_ref=outbox.at[f, pl.ds(1, ntok - 1), :, cols],
            dst_ref=inbox.at[f, pl.ds(1, ntok - 1), :, cols],
            send_sem=fac_send.at[f, c],
            recv_sem=fac_recv.at[f, c],
            device_id={"tok": lax.rem(mine + 1, ntok)},
            device_id_type=MESH,
        )

    def tok_copy(f, i):
        return pltpu.make_async_remote_copy(
            src_ref=sources[f],
            dst_ref=tokens.at[f, pl.ds(half_row, rows_dev), :],
            send_sem=tok_send.at[f, i],
            recv_sem=tok_recv.at[f, i],
            device_id={"sub": lax.rem(half + i, nsub)},
            device_id_type=MESH,
        )

    def part_copy(f, i):
        place, device = quad_device(i)
        return pltpu.make_async_remote_copy(
            src_ref=acc.at[f, pl.ds(pl.multiple_of(place * share, 8), share), :],
            dst_ref=parts.at[f, i],
            send_sem=part_send.at[f, i],
            recv_sem=part_recv.at[f, i],
            device_id=device,
            device_id_type=MESH,
        )

    pieces = [(f, c) for f in range(2) for c in range(chunks)]
    ahead = 4
    lag = 3 if lean else 0
    pack(0)
    pl.semaphore_wait(barrier, ntok - 1 + nquad - 1)
    for f, c in pieces[:ahead]:
        fac_start(f, c)
    for i in range(1, nsub):
        tok_copy(0, i).start()
    for i in range(1, nsub):
        tok_copy(1, i).start()
    pack(1)

    step = 16

    def split(f, base):
        @pl.loop(0, rows_dev // step)
        def _(b):
            rows = pl.ds(pl.multiple_of(base + b * step, step), step)
            value = tokens[f, rows, :]
            top = value.astype(jnp.bfloat16)
            high[f, rows, :] = top
            low[f, rows, :] = (value - top.astype(jnp.float32)).astype(jnp.bfloat16)

    tile = 128

    def multiply(f, c):
        cols = pl.ds(c * piece, piece)

        @pl.loop(0, block_rows // tile)
        def _(b):
            rows = pl.ds(pl.multiple_of(b * tile, tile), tile)
            weight = inbox[f, :, :, cols].reshape(places * seats * rank, piece)
            dims = (((1,), (1,)), ((), ()))
            value = lax.dot_general(
                high[f, rows, cols], weight, dims, preferred_element_type=jnp.float32
            ) + lax.dot_general(
                low[f, rows, cols], weight, dims, preferred_element_type=jnp.float32
            )
            if c == 0:
                acc[f, rows, :] = value
            else:
                acc[f, rows, :] += value

    if lean:
        forward(*pieces[0])
    for f in range(2):
        loads[f].wait()
        split(f, half * rows_dev)
        if lean:
            forward(*pieces[1 + f])

    lists = lists_ref[...]
    lane1 = lax.broadcasted_iota(jnp.int32, (8, lanes), 1)
    arrived = jnp.zeros((8, lanes), jnp.int32)
    label = jnp.zeros((8, lanes), jnp.int32)
    for k in range(topc):
        hit = (jnp.broadcast_to(lists[k : k + 1], (8, lanes)) == mine) & (lane1 < ntok * local_q)
        arrived = jnp.where(hit, 1, arrived)
        label = jnp.where(hit, jnp.broadcast_to(lists[topc + k : topc + k + 1], (8, lanes)), label)
    slot = jnp.zeros((8, lanes), jnp.int32)
    for a in range(1, local_q):
        slot = slot + jnp.where(
            lax.rem(lane1, local_q) >= a, pltpu.roll(arrived, a, axis=1), 0
        )
    width = places * seats * rank
    place = lax.broadcasted_iota(jnp.int32, (width, lanes), 0)
    query = lax.broadcasted_iota(jnp.int32, (width, lanes), 1)
    spot = lax.div(place, seats * rank)
    origin = lax.rem(mine - spot + 2 * ntok, ntok)
    source = lax.div(query, local_q)
    seat = lax.rem(lax.div(place, rank), seats)
    chosen = (slot[0:1] == seat) & (source == origin) & (spot < ntok)
    if lean:
        passed = (
            ((spot == ntok) & (source < mine))
            | ((spot == ntok + 1) & (source > mine))
            | ((spot == ntok + 2) & (source == mine))
        )
        chosen = chosen | ((slot[0:1] == 1) & passed)
    chosen = (arrived[0:1] == 1) & chosen
    mapping = chosen.astype(jnp.float32)
    base = quad * share
    wide = tc_ref.shape[0]
    row = lax.broadcasted_iota(jnp.int32, (share, wide), 0) + base
    other = lax.broadcasted_iota(jnp.int32, (share, wide), 1)
    row_cluster = jnp.sum(
        jnp.where(row == other, tc_ref[...].reshape(1, wide), 0).astype(jnp.float32), axis=1, keepdims=True
    )
    spot = lax.broadcasted_iota(jnp.int32, (share, lanes), 0) + base
    owner = lax.div(spot, rows_dev)
    limit = jnp.zeros((share, lanes), jnp.int32)
    for i in range(nsub):
        limit = jnp.where(owner == i, cnt_ref[mine * nsub + i], limit)
    live = (lax.rem(spot, rows_dev) < limit) & (row_cluster == label[0:1].astype(jnp.float32))
    live = live.astype(jnp.float32)

    for p, (f, c) in enumerate(pieces):
        if lean and p + lag < len(pieces):
            forward(*pieces[p + lag])
        if c == 0:
            for i in range(1, nsub):
                tok_copy(f, i).wait()
                split(f, lax.rem(half + nsub - i, nsub) * rows_dev)
        fac_all(f, c).wait_recv()
        if p + ahead < len(pieces):
            fac_start(*pieces[p + ahead])
        multiply(f, c)
        if c == chunks - 1:
            for i in range(1, nquad):
                part_copy(f, i).start()

    def total(f, h):
        start = pl.multiple_of(quad * share, 8)
        value = acc[f, pl.ds(start, share), :] if h == 0 else parts[f, h]
        for i in range(h + nsub, nquad, nsub):
            value = value + parts[f, i]
        return value

    for i in range(1, nquad):
        part_copy(0, i).wait_recv()
    for i in range(1, nquad):
        part_copy(1, i).wait_recv()
    product = total(0, 0) * total(1, 0)
    for h in range(1, nsub):
        product = product + total(0, h) * total(1, h)
    result = live * lax.dot_general(
        product,
        mapping,
        (((1,), (0,)), ((), ())),
        precision=lax.Precision.HIGHEST,
        preferred_element_type=jnp.float32,
    )
    out_ref[...] = result.T[: out_ref.shape[0], :]

    for f in range(2):
        for c in range(chunks):
            fac_all(f, c).wait_send()
        for i in range(1, nquad):
            part_copy(f, i).wait_send()
    if lean:
        for f, c in pieces:
            for way, ends in ((0, last), (1, first)):

                @pl.when(jnp.logical_not(ends))
                def _():
                    relay_copy(f, c, way).wait_send()


def on_device(
    activation,
    cotangent,
    query_output_factor,
    query_input_factor,
    query_dest,
    query_cluster,
    token_cluster,
    token_count,
):
    ntok = lax.axis_size("tok")
    nsub = lax.axis_size("sub")
    nwide = lax.axis_size("width")
    local_q, topc = query_dest.shape
    rows_dev, depth = activation.shape
    rank = query_output_factor.shape[1]
    block_rows = rows_dev * nsub
    nquad = nwide * nsub
    share = block_rows // nquad
    lanes = -(-ntok * local_q // 128) * 128
    lines = -(-2 * topc // 8) * 8
    ngroup = lax.axis_size("groups")
    chunks = 4
    dma = pltpu.SemaphoreType.DMA
    vmem = pl.BlockSpec(memory_space=pltpu.VMEM)
    smem = pl.BlockSpec(memory_space=pltpu.SMEM)
    hbm = pl.BlockSpec(memory_space=pl.ANY)
    dest, clus = query_dest.T, query_cluster.T
    lists, count = pl.pallas_call(
        functools.partial(meta_kernel, ngroup, ntok),
        out_shape=(
            jax.ShapeDtypeStruct((lines, lanes), jnp.int32),
            jax.ShapeDtypeStruct((1,), jnp.int32),
        ),
        in_specs=[smem, smem],
        out_specs=(vmem, smem),
        scratch_shapes=[
            pltpu.VMEM((lines, lanes), jnp.int32),
            pltpu.VMEM((ngroup * ntok, lines, lanes), jnp.int32),
            dma((ngroup * ntok,)),
            dma((ngroup * ntok,)),
        ],
        compiler_params=pltpu.CompilerParams(collective_id=0, has_side_effects=True),
    )(dest, clus)

    def call(lean, *args):
        seats = 1 if lean else CAP
        places = ntok + 4 if lean else ntok
        width = places * seats * rank
        return pl.pallas_call(
            functools.partial(kernel, ntok, nwide, nsub, chunks, lean),
            out_shape=jax.ShapeDtypeStruct((ntok * local_q, share), jnp.float32),
            in_specs=[hbm, hbm, vmem, vmem, smem, vmem, vmem, smem],
            out_specs=vmem,
            scratch_shapes=[
                pltpu.VMEM((2, block_rows, depth), jnp.float32),
                pltpu.VMEM((2, block_rows, depth), jnp.bfloat16),
                pltpu.VMEM((2, block_rows, depth), jnp.bfloat16),
                pltpu.VMEM((2, ntok, seats * rank, depth), jnp.bfloat16),
                pltpu.VMEM((2, places, seats * rank, depth), jnp.bfloat16),
                pltpu.VMEM((2, block_rows, width), jnp.float32),
                pltpu.VMEM((2, nquad, share, width), jnp.float32),
                pltpu.VMEM((2, 2, rank, depth), jnp.bfloat16),
                dma((2,)),
                dma((2, nsub)),
                dma((2, nsub)),
                dma((2, 2, chunks)),
                dma((2, 2, chunks)),
                dma((2, chunks)),
                dma((2, chunks)),
                dma((2, nquad)),
                dma((2, nquad)),
            ],
            compiler_params=pltpu.CompilerParams(
                collective_id=1 if lean else 2,
                has_side_effects=True,
                vmem_limit_bytes=56 * 2**20,
            ),
        )(*args)

    scores = lax.cond(
        count[0] <= 1,
        functools.partial(call, True),
        functools.partial(call, False),
        activation,
        cotangent,
        query_output_factor,
        query_input_factor,
        dest,
        lists,
        token_cluster,
        token_count,
    )
    return scores.T


def solution(mesh):
    placed = (
        P(("groups", "tok", "sub"), "width"),
        P(("groups", "tok", "sub"), "width"),
        P(("groups", "tok"), "sub", "width"),
        P(("groups", "tok"), "sub", "width"),
        P(("groups", "tok"), None),
        P(("groups", "tok"), None),
        P(("groups", "tok")),
        P("groups"),
    )
    return jax.shard_map(
        on_device,
        mesh=mesh,
        in_specs=placed,
        out_specs=P(("groups", "tok", "width", "sub"), None),
        check_vma=False,
    )
```

```python
import functools

import jax
import jax.numpy as jnp
from jax import lax
from jax.experimental import pallas as pl
from jax.experimental.pallas import tpu as pltpu
from jax.sharding import PartitionSpec as P

CAP = 2
MESH = pl.DeviceIdType.MESH


def kernel(
    ntok,
    nwide,
    nsub,
    chunks,
    act_hbm,
    cot_hbm,
    u_ref,
    v_ref,
    dest_ref,
    clus_ref,
    tc_ref,
    cnt_ref,
    out_ref,
    tokens,
    high,
    low,
    outbox,
    inbox,
    acc,
    parts,
    meta_out,
    meta_in,
    load_sem,
    tok_send,
    tok_recv,
    meta_send,
    meta_recv,
    fac_send,
    fac_recv,
    part_send,
    part_recv,
):
    mine = lax.axis_index("tok")
    column = lax.axis_index("width")
    half = lax.axis_index("sub")
    topc, local_q = dest_ref.shape
    rows_dev, depth = act_hbm.shape
    block_rows = rows_dev * nsub
    rank = u_ref.shape[1]
    lanes = meta_out.shape[1]
    piece = depth // chunks
    nquad = nwide * nsub
    quad = column * nsub + half
    share = block_rows // nquad
    sources = (cot_hbm, act_hbm)
    factors = (u_ref, v_ref)
    half_row = pl.multiple_of(half * rows_dev, 8)

    def quad_device(offset):
        place = lax.rem(quad + offset, nquad)
        return place, {"width": lax.div(place, nsub), "sub": lax.rem(place, nsub)}

    barrier = pltpu.get_barrier_semaphore()
    for j in range(1, ntok):
        pl.semaphore_signal(
            barrier, inc=1, device_id={"tok": lax.rem(mine + j, ntok)}, device_id_type=MESH
        )
    for i in range(1, nquad):
        pl.semaphore_signal(barrier, inc=1, device_id=quad_device(i)[1], device_id_type=MESH)

    loads = [
        pltpu.make_async_copy(
            sources[f], tokens.at[f, pl.ds(half_row, rows_dev), :], load_sem.at[f]
        )
        for f in range(2)
    ]
    for load in loads:
        load.start()

    line = lax.broadcasted_iota(jnp.int32, meta_out.shape, 0)
    lane = lax.broadcasted_iota(jnp.int32, meta_out.shape, 1)
    meta = jnp.zeros(meta_out.shape, jnp.int32)
    for a in range(local_q):
        here = lane == mine * local_q + a
        for k in range(topc):
            meta = jnp.where(here & (line == k), dest_ref[k, a], meta)
            meta = jnp.where(here & (line == topc + k), clus_ref[k, a], meta)
    meta_out[...] = meta
    meta_in[0] = meta

    def picked(target):
        seen = jnp.int32(0)
        found = [jnp.int32(0) for _ in range(CAP)]
        for a in range(local_q):
            named = dest_ref[0, a] == target
            for k in range(1, topc):
                named = jnp.logical_or(named, dest_ref[k, a] == target)
            for e in range(CAP):
                found[e] = jnp.where(jnp.logical_and(named, seen == e), a, found[e])
            seen = seen + named.astype(jnp.int32)
        return found

    def pack(f):
        def one(j, carry):
            found = picked(lax.rem(mine + j, ntok))
            for e in range(CAP):
                outbox[f, j, e * rank : (e + 1) * rank, :] = factors[f][found[e]]
            return carry

        lax.fori_loop(1, ntok, one, 0)
        found = picked(mine)
        for e in range(CAP):
            inbox[f, 0, e * rank : (e + 1) * rank, :] = factors[f][found[e]]

    def fac_copy(f, c, j):
        cols = pl.ds(c * piece, piece)
        return pltpu.make_async_remote_copy(
            src_ref=outbox.at[f, j, :, cols],
            dst_ref=inbox.at[f, j, :, cols],
            send_sem=fac_send.at[f, c],
            recv_sem=fac_recv.at[f, c],
            device_id={"tok": lax.rem(mine + j, ntok)},
            device_id_type=MESH,
        )

    def fac_start(f, c):
        def one(j, carry):
            fac_copy(f, c, j).start()
            return carry

        lax.fori_loop(1, ntok, one, 0)

    def fac_all(f, c):
        cols = pl.ds(c * piece, piece)
        return pltpu.make_async_remote_copy(
            src_ref=outbox.at[f, pl.ds(1, ntok - 1), :, cols],
            dst_ref=inbox.at[f, pl.ds(1, ntok - 1), :, cols],
            send_sem=fac_send.at[f, c],
            recv_sem=fac_recv.at[f, c],
            device_id={"tok": lax.rem(mine + 1, ntok)},
            device_id_type=MESH,
        )

    def meta_copy(j):
        return pltpu.make_async_remote_copy(
            src_ref=meta_out,
            dst_ref=meta_in.at[j],
            send_sem=meta_send.at[j],
            recv_sem=meta_recv.at[j],
            device_id={"tok": lax.rem(mine + j, ntok)},
            device_id_type=MESH,
        )

    def tok_copy(f, i):
        return pltpu.make_async_remote_copy(
            src_ref=sources[f],
            dst_ref=tokens.at[f, pl.ds(half_row, rows_dev), :],
            send_sem=tok_send.at[f, i],
            recv_sem=tok_recv.at[f, i],
            device_id={"sub": lax.rem(half + i, nsub)},
            device_id_type=MESH,
        )

    def part_copy(f, i):
        place, device = quad_device(i)
        return pltpu.make_async_remote_copy(
            src_ref=acc.at[f, pl.ds(pl.multiple_of(place * share, 8), share), :],
            dst_ref=parts.at[f, i],
            send_sem=part_send.at[f, i],
            recv_sem=part_recv.at[f, i],
            device_id=device,
            device_id_type=MESH,
        )

    pack(0)
    pl.semaphore_wait(barrier, ntok - 1 + nquad - 1)
    for c in range(chunks):
        fac_start(0, c)
    for i in range(1, nsub):
        tok_copy(0, i).start()

    def meta_go(j, carry):
        meta_copy(j).start()
        return carry

    lax.fori_loop(1, ntok, meta_go, 0)
    for i in range(1, nsub):
        tok_copy(1, i).start()
    pack(1)

    step = 16

    def split(f, base):
        @pl.loop(0, rows_dev // step)
        def _(b):
            rows = pl.ds(pl.multiple_of(base + b * step, step), step)
            value = tokens[f, rows, :]
            top = value.astype(jnp.bfloat16)
            high[f, rows, :] = top
            low[f, rows, :] = (value - top.astype(jnp.float32)).astype(jnp.bfloat16)

    tile = 128

    def multiply(f, c):
        cols = pl.ds(c * piece, piece)

        @pl.loop(0, block_rows // tile)
        def _(b):
            rows = pl.ds(pl.multiple_of(b * tile, tile), tile)
            weight = inbox[f, :, :, cols].reshape(ntok * CAP * rank, piece)
            dims = (((1,), (1,)), ((), ()))
            value = lax.dot_general(
                high[f, rows, cols], weight, dims, preferred_element_type=jnp.float32
            ) + lax.dot_general(
                low[f, rows, cols], weight, dims, preferred_element_type=jnp.float32
            )
            if c == 0:
                acc[f, rows, :] = value
            else:
                acc[f, rows, :] += value

    for f in range(2):
        loads[f].wait()
        split(f, half * rows_dev)

    def meta_wait(j, carry):
        meta_copy(j).wait()
        return carry

    lax.fori_loop(1, ntok, meta_wait, 0)
    lists = jnp.sum(meta_in[...], axis=0)
    lane1 = lax.broadcasted_iota(jnp.int32, (8, lanes), 1)
    arrived = jnp.zeros((8, lanes), jnp.int32)
    label = jnp.zeros((8, lanes), jnp.int32)
    for k in range(topc):
        hit = (jnp.broadcast_to(lists[k : k + 1], (8, lanes)) == mine) & (lane1 < ntok * local_q)
        arrived = jnp.where(hit, 1, arrived)
        label = jnp.where(hit, jnp.broadcast_to(lists[topc + k : topc + k + 1], (8, lanes)), label)
    slot = jnp.zeros((8, lanes), jnp.int32)
    for a in range(1, local_q):
        slot = slot + jnp.where(
            lax.rem(lane1, local_q) >= a, pltpu.roll(arrived, a, axis=1), 0
        )
    width = ntok * CAP * rank
    place = lax.broadcasted_iota(jnp.int32, (width, lanes), 0)
    query = lax.broadcasted_iota(jnp.int32, (width, lanes), 1)
    origin = lax.rem(mine - lax.div(place, CAP * rank) + ntok, ntok)
    seat = lax.rem(lax.div(place, rank), CAP)
    chosen = (
        (arrived[0:1] == 1) & (slot[0:1] == seat) & (lax.div(query, local_q) == origin)
    )
    mapping = chosen.astype(jnp.float32)
    base = quad * share
    wide = tc_ref.shape[0]
    row = lax.broadcasted_iota(jnp.int32, (share, wide), 0) + base
    other = lax.broadcasted_iota(jnp.int32, (share, wide), 1)
    row_cluster = jnp.sum(
        jnp.where(row == other, tc_ref[...].reshape(1, wide), 0).astype(jnp.float32), axis=1, keepdims=True
    )
    spot = lax.broadcasted_iota(jnp.int32, (share, lanes), 0) + base
    owner = lax.div(spot, rows_dev)
    limit = jnp.zeros((share, lanes), jnp.int32)
    for i in range(nsub):
        limit = jnp.where(owner == i, cnt_ref[mine * nsub + i], limit)
    live = (lax.rem(spot, rows_dev) < limit) & (row_cluster == label[0:1].astype(jnp.float32))
    live = live.astype(jnp.float32)

    for f in range(2):
        for i in range(1, nsub):
            tok_copy(f, i).wait()
            split(f, lax.rem(half + nsub - i, nsub) * rows_dev)
        for c in range(chunks):
            fac_all(f, c).wait_recv()
            if f == 0:
                fac_start(1, c)
            multiply(f, c)
        for i in range(1, nquad):
            part_copy(f, i).start()

    def total(f, h):
        start = pl.multiple_of(quad * share, 8)
        value = acc[f, pl.ds(start, share), :] if h == 0 else parts[f, h]
        for i in range(h + nsub, nquad, nsub):
            value = value + parts[f, i]
        return value

    for i in range(1, nquad):
        part_copy(0, i).wait_recv()
    for i in range(1, nquad):
        part_copy(1, i).wait_recv()
    product = total(0, 0) * total(1, 0)
    for h in range(1, nsub):
        product = product + total(0, h) * total(1, h)
    result = live * lax.dot_general(
        product,
        mapping,
        (((1,), (0,)), ((), ())),
        precision=lax.Precision.HIGHEST,
        preferred_element_type=jnp.float32,
    )
    out_ref[...] = result.T[: out_ref.shape[0], :]

    for f in range(2):
        for c in range(chunks):
            fac_all(f, c).wait_send()
        for i in range(1, nquad):
            part_copy(f, i).wait_send()


def on_device(
    activation,
    cotangent,
    query_output_factor,
    query_input_factor,
    query_dest,
    query_cluster,
    token_cluster,
    token_count,
):
    ntok = lax.axis_size("tok")
    nsub = lax.axis_size("sub")
    nwide = lax.axis_size("width")
    local_q, topc = query_dest.shape
    rows_dev, depth = activation.shape
    rank = query_output_factor.shape[1]
    block_rows = rows_dev * nsub
    nquad = nwide * nsub
    share = block_rows // nquad
    lanes = -(-ntok * local_q // 128) * 128
    lines = -(-2 * topc // 8) * 8
    width = ntok * CAP * rank
    chunks = 2
    dma = pltpu.SemaphoreType.DMA
    vmem = pl.BlockSpec(memory_space=pltpu.VMEM)
    smem = pl.BlockSpec(memory_space=pltpu.SMEM)
    hbm = pl.BlockSpec(memory_space=pl.ANY)
    return pl.pallas_call(
        functools.partial(kernel, ntok, nwide, nsub, chunks),
        out_shape=jax.ShapeDtypeStruct((ntok * local_q, share), jnp.float32),
        in_specs=[hbm, hbm, vmem, vmem, smem, smem, vmem, smem],
        out_specs=vmem,
        scratch_shapes=[
            pltpu.VMEM((2, block_rows, depth), jnp.float32),
            pltpu.VMEM((2, block_rows, depth), jnp.bfloat16),
            pltpu.VMEM((2, block_rows, depth), jnp.bfloat16),
            pltpu.VMEM((2, ntok, CAP * rank, depth), jnp.bfloat16),
            pltpu.VMEM((2, ntok, CAP * rank, depth), jnp.bfloat16),
            pltpu.VMEM((2, block_rows, width), jnp.float32),
            pltpu.VMEM((2, nquad, share, width), jnp.float32),
            pltpu.VMEM((lines, lanes), jnp.int32),
            pltpu.VMEM((ntok, lines, lanes), jnp.int32),
            dma((2,)),
            dma((2, nsub)),
            dma((2, nsub)),
            dma((ntok,)),
            dma((ntok,)),
            dma((2, chunks)),
            dma((2, chunks)),
            dma((2, nquad)),
            dma((2, nquad)),
        ],
        compiler_params=pltpu.CompilerParams(
            collective_id=0, has_side_effects=True, vmem_limit_bytes=56 * 2**20
        ),
    )(
        activation,
        cotangent,
        query_output_factor,
        query_input_factor,
        query_dest.T,
        query_cluster.T,
        token_cluster,
        token_count,
    ).T


def solution(mesh):
    placed = (
        P(("groups", "tok", "sub"), "width"),
        P(("groups", "tok", "sub"), "width"),
        P(("groups", "tok"), "sub", "width"),
        P(("groups", "tok"), "sub", "width"),
        P(("groups", "tok"), None),
        P(("groups", "tok"), None),
        P(("groups", "tok")),
        P("groups"),
    )
    return jax.shard_map(
        on_device,
        mesh=mesh,
        in_specs=placed,
        out_specs=P(("groups", "tok", "width", "sub"), None),
        check_vma=False,
    )
```

```python
import functools

import jax
import jax.numpy as jnp
from jax import lax
from jax.experimental import pallas as pl
from jax.experimental.pallas import tpu as pltpu
from jax.sharding import PartitionSpec as P

CAP = 2
CHUNKS = 4
AHEAD = 3
MESH = pl.DeviceIdType.MESH


def over_lanes(lists, topc, local_q, count):
    shape = (8, lists.shape[1])
    lane = lax.broadcasted_iota(jnp.int32, shape, 1)
    named = [jnp.broadcast_to(lists[k : k + 1], shape) for k in range(topc)]
    total = jnp.zeros(shape, jnp.int32)
    for k in range(topc):
        again = jnp.zeros(shape, jnp.int32)
        for a in range(1, local_q):
            earlier = (lax.rem(lane, local_q) >= a) & (lane < count)
            for other in range(topc):
                same = named[k] == pltpu.roll(named[other], a, axis=1)
                again = jnp.where(earlier & same, 1, again)
        total = total + again
    return total


def meta_kernel(
    ngroup, ntok, dest_ref, clus_ref, lists_ref, count_ref, meta_out, meta_in, send, recv
):
    group = lax.axis_index("groups")
    mine = lax.axis_index("tok")
    topc, local_q = dest_ref.shape
    everyone = ngroup * ntok

    def device(p):
        return {
            "groups": lax.rem(group + lax.div(p, ntok), ngroup),
            "tok": lax.rem(mine + lax.rem(p, ntok), ntok),
        }

    barrier = pltpu.get_barrier_semaphore()

    def greet(p, carry):
        pl.semaphore_signal(barrier, inc=1, device_id=device(p), device_id_type=MESH)
        return carry

    lax.fori_loop(1, everyone, greet, 0)
    line = lax.broadcasted_iota(jnp.int32, meta_out.shape, 0)
    lane = lax.broadcasted_iota(jnp.int32, meta_out.shape, 1)
    meta = jnp.zeros(meta_out.shape, jnp.int32)
    for a in range(local_q):
        here = lane == mine * local_q + a
        for k in range(topc):
            meta = jnp.where(here & (line == k), dest_ref[k, a], meta)
            meta = jnp.where(here & (line == topc + k), clus_ref[k, a], meta)
    meta_out[...] = meta
    meta_in[0] = meta
    pl.semaphore_wait(barrier, everyone - 1)

    def copy(p):
        return pltpu.make_async_remote_copy(
            src_ref=meta_out,
            dst_ref=meta_in.at[p],
            send_sem=send.at[p],
            recv_sem=recv.at[p],
            device_id=device(p),
            device_id_type=MESH,
        )

    def go(p, carry):
        copy(p).start()
        return carry

    def done(p, carry):
        copy(p).wait()
        return carry

    lax.fori_loop(1, everyone, go, 0)
    lax.fori_loop(1, everyone, done, 0)
    most = jnp.float32(0)
    for g in range(ngroup):
        lists = jnp.sum(meta_in[g * ntok : (g + 1) * ntok], axis=0)
        if g == 0:
            lists_ref[...] = lists
        over = over_lanes(lists, topc, local_q, ntok * local_q)
        most = jnp.maximum(most, jnp.sum(over[0:1].astype(jnp.float32)))
    count_ref[0] = most.astype(jnp.int32)


def kernel(
    ntok,
    nwide,
    nsub,
    chunks,
    lean,
    act_hbm,
    cot_hbm,
    u_ref,
    v_ref,
    dest_ref,
    lists_ref,
    tc_ref,
    cnt_ref,
    out_ref,
    tokens,
    high,
    low,
    outbox,
    inbox,
    acc,
    parts,
    relay,
    load_sem,
    tok_send,
    tok_recv,
    relay_send,
    relay_recv,
    fac_send,
    fac_recv,
    part_send,
    part_recv,
):
    mine = lax.axis_index("tok")
    column = lax.axis_index("width")
    half = lax.axis_index("sub")
    topc, local_q = dest_ref.shape
    rows_dev, depth = act_hbm.shape
    block_rows = rows_dev * nsub
    rank = u_ref.shape[1]
    lanes = lists_ref.shape[1]
    seats = 1 if lean else CAP
    places = inbox.shape[1]
    piece = depth // chunks
    nquad = nwide * nsub
    quad = column * nsub + half
    share = block_rows // nquad
    sources = (cot_hbm, act_hbm)
    factors = (u_ref, v_ref)
    half_row = pl.multiple_of(half * rows_dev, 8)

    def quad_device(offset):
        place = lax.rem(quad + offset, nquad)
        return place, {"width": lax.div(place, nsub), "sub": lax.rem(place, nsub)}

    pieces = [(f, c) for f in range(2) for c in range(chunks)]
    barrier = pltpu.get_barrier_semaphore()
    for j in range(1, ntok):
        pl.semaphore_signal(
            barrier, inc=1, device_id={"tok": lax.rem(mine + j, ntok)}, device_id_type=MESH
        )
    for i in range(1, nquad):
        pl.semaphore_signal(barrier, inc=1, device_id=quad_device(i)[1], device_id_type=MESH)

    loads = [
        pltpu.make_async_copy(
            sources[f], tokens.at[f, pl.ds(half_row, rows_dev), :], load_sem.at[f]
        )
        for f in range(2)
    ]
    for load in loads:
        load.start()

    def picked(target):
        seen = jnp.int32(0)
        found = [jnp.int32(0) for _ in range(CAP)]
        for a in range(local_q):
            named = dest_ref[0, a] == target
            for k in range(1, topc):
                named = jnp.logical_or(named, dest_ref[k, a] == target)
            for e in range(CAP):
                found[e] = jnp.where(jnp.logical_and(named, seen == e), a, found[e])
            seen = seen + named.astype(jnp.int32)
        return found

    extra = jnp.int32(0)
    holds = jnp.int32(0)
    for a in range(1, local_q):
        for before in range(a):
            for k in range(topc):
                for other in range(topc):
                    same = dest_ref[k, a] == dest_ref[other, before]
                    extra = jnp.where(same, a, extra)
                    holds = jnp.where(same, 1, holds)

    def relay_copy(f, c, way):
        cols = pl.ds(c * piece, piece)
        step = 1 if way == 0 else ntok - 1
        return pltpu.make_async_remote_copy(
            src_ref=relay.at[way, f, :, cols],
            dst_ref=inbox.at[f, ntok + way, :, cols],
            send_sem=relay_send.at[way, f, c],
            recv_sem=relay_recv.at[way, f, c],
            device_id={"tok": lax.rem(mine + step, ntok)},
            device_id_type=MESH,
        )

    first, last = mine == 0, mine == ntok - 1

    def relay_send_on(f, c, way, starts):
        cols = pl.ds(c * piece, piece)
        mask = holds == 1
        if starts:
            relay[way, f, :, cols] = inbox[f, ntok + 2, :, cols]
        else:
            relay_copy(f, c, way).wait_recv()
            relay[way, f, :, cols] = jnp.where(
                mask, inbox[f, ntok + 2, :, cols], inbox[f, ntok + way, :, cols]
            )
        relay_copy(f, c, way).start()

    def begin(f, c):
        @pl.when(first)
        def _():
            relay_send_on(f, c, 0, True)

        @pl.when(last)
        def _():
            relay_send_on(f, c, 1, True)

    inner = jnp.logical_not(jnp.logical_or(first, last))
    lower = mine < ntok // 2

    def forward(turn):
        for way in range(2):
            near = lower if way == turn else jnp.logical_not(lower)

            @pl.when(jnp.logical_and(inner, near))
            def _():
                for f, c in pieces:
                    relay_send_on(f, c, way, False)

    def arrive(f, c):
        @pl.when(last)
        def _():
            relay_copy(f, c, 0).wait_recv()

        @pl.when(first)
        def _():
            relay_copy(f, c, 1).wait_recv()

    def pack(f):
        def one(j, carry):
            found = picked(lax.rem(mine + j, ntok))
            for e in range(seats):
                outbox[f, j, e * rank : (e + 1) * rank, :] = factors[f][found[e]]
            return carry

        lax.fori_loop(1, ntok, one, 0)
        found = picked(mine)
        for e in range(seats):
            inbox[f, 0, e * rank : (e + 1) * rank, :] = factors[f][found[e]]
        if lean:
            value = factors[f][extra]
            inbox[f, ntok + 2] = value
            inbox[f, ntok + 3] = value

            @pl.when(mine == 0)
            def _():
                inbox[f, ntok] = jnp.zeros_like(value)

            @pl.when(mine == ntok - 1)
            def _():
                inbox[f, ntok + 1] = jnp.zeros_like(value)

    def fac_copy(f, c, j):
        cols = pl.ds(c * piece, piece)
        return pltpu.make_async_remote_copy(
            src_ref=outbox.at[f, j, :, cols],
            dst_ref=inbox.at[f, j, :, cols],
            send_sem=fac_send.at[f, c],
            recv_sem=fac_recv.at[f, c],
            device_id={"tok": lax.rem(mine + j, ntok)},
            device_id_type=MESH,
        )

    def fac_start(f, c):
        def one(j, carry):
            fac_copy(f, c, j).start()
            return carry

        lax.fori_loop(1, ntok, one, 0)

    def fac_all(f, c):
        cols = pl.ds(c * piece, piece)
        return pltpu.make_async_remote_copy(
            src_ref=outbox.at[f, pl.ds(1, ntok - 1), :, cols],
            dst_ref=inbox.at[f, pl.ds(1, ntok - 1), :, cols],
            send_sem=fac_send.at[f, c],
            recv_sem=fac_recv.at[f, c],
            device_id={"tok": lax.rem(mine + 1, ntok)},
            device_id_type=MESH,
        )

    def tok_copy(f, i):
        return pltpu.make_async_remote_copy(
            src_ref=sources[f],
            dst_ref=tokens.at[f, pl.ds(half_row, rows_dev), :],
            send_sem=tok_send.at[f, i],
            recv_sem=tok_recv.at[f, i],
            device_id={"sub": lax.rem(half + i, nsub)},
            device_id_type=MESH,
        )

    def part_copy(f, i):
        place, device = quad_device(i)
        return pltpu.make_async_remote_copy(
            src_ref=acc.at[f, pl.ds(pl.multiple_of(place * share, 8), share), :],
            dst_ref=parts.at[f, i],
            send_sem=part_send.at[f, i],
            recv_sem=part_recv.at[f, i],
            device_id=device,
            device_id_type=MESH,
        )

    ahead = AHEAD
    pack(0)
    pack(1)
    pl.semaphore_wait(barrier, ntok - 1 + nquad - 1)
    if lean:
        for f, c in pieces:
            begin(f, c)
        forward(0)
        forward(1)
    for f, c in pieces[:ahead]:
        fac_start(f, c)
    for i in range(1, nsub):
        tok_copy(0, i).start()
    for i in range(1, nsub):
        tok_copy(1, i).start()

    step = 16

    def split(f, base):
        @pl.loop(0, rows_dev // step)
        def _(b):
            rows = pl.ds(pl.multiple_of(base + b * step, step), step)
            value = tokens[f, rows, :]
            top = value.astype(jnp.bfloat16)
            high[f, rows, :] = top
            low[f, rows, :] = (value - top.astype(jnp.float32)).astype(jnp.bfloat16)

    tile = 128

    def multiply(f, c):
        cols = pl.ds(c * piece, piece)

        @pl.loop(0, block_rows // tile)
        def _(b):
            rows = pl.ds(pl.multiple_of(b * tile, tile), tile)
            weight = inbox[f, :, :, cols].reshape(places * seats * rank, piece)
            dims = (((1,), (1,)), ((), ()))
            value = lax.dot_general(
                high[f, rows, cols], weight, dims, preferred_element_type=jnp.float32
            ) + lax.dot_general(
                low[f, rows, cols], weight, dims, preferred_element_type=jnp.float32
            )
            if c == 0:
                acc[f, rows, :] = value
            else:
                acc[f, rows, :] += value

    for f in range(2):
        loads[f].wait()
        split(f, half * rows_dev)

    lists = lists_ref[...]
    lane1 = lax.broadcasted_iota(jnp.int32, (8, lanes), 1)
    arrived = jnp.zeros((8, lanes), jnp.int32)
    label = jnp.zeros((8, lanes), jnp.int32)
    for k in range(topc):
        hit = (jnp.broadcast_to(lists[k : k + 1], (8, lanes)) == mine) & (lane1 < ntok * local_q)
        arrived = jnp.where(hit, 1, arrived)
        label = jnp.where(hit, jnp.broadcast_to(lists[topc + k : topc + k + 1], (8, lanes)), label)
    slot = jnp.zeros((8, lanes), jnp.int32)
    for a in range(1, local_q):
        slot = slot + jnp.where(
            lax.rem(lane1, local_q) >= a, pltpu.roll(arrived, a, axis=1), 0
        )
    width = places * seats * rank
    place = lax.broadcasted_iota(jnp.int32, (width, lanes), 0)
    query = lax.broadcasted_iota(jnp.int32, (width, lanes), 1)
    spot = lax.div(place, seats * rank)
    origin = lax.rem(mine - spot + 2 * ntok, ntok)
    source = lax.div(query, local_q)
    seat = lax.rem(lax.div(place, rank), seats)
    chosen = (slot[0:1] == seat) & (source == origin) & (spot < ntok)
    if lean:
        passed = (
            ((spot == ntok) & (source < mine))
            | ((spot == ntok + 1) & (source > mine))
            | ((spot == ntok + 2) & (source == mine))
        )
        chosen = chosen | ((slot[0:1] == 1) & passed)
    chosen = (arrived[0:1] == 1) & chosen
    mapping = chosen.astype(jnp.float32)
    base = quad * share
    wide = tc_ref.shape[0]
    row = lax.broadcasted_iota(jnp.int32, (share, wide), 0) + base
    other = lax.broadcasted_iota(jnp.int32, (share, wide), 1)
    row_cluster = jnp.sum(
        jnp.where(row == other, tc_ref[...].reshape(1, wide), 0).astype(jnp.float32), axis=1, keepdims=True
    )
    spot = lax.broadcasted_iota(jnp.int32, (share, lanes), 0) + base
    owner = lax.div(spot, rows_dev)
    limit = jnp.zeros((share, lanes), jnp.int32)
    for i in range(nsub):
        limit = jnp.where(owner == i, cnt_ref[mine * nsub + i], limit)
    live = (lax.rem(spot, rows_dev) < limit) & (row_cluster == label[0:1].astype(jnp.float32))
    live = live.astype(jnp.float32)

    for p, (f, c) in enumerate(pieces):
        fac_all(f, c).wait_recv()
        if p + ahead < len(pieces):
            fac_start(*pieces[p + ahead])
        if c == 0:
            for i in range(1, nsub):
                tok_copy(f, i).wait()
                split(f, lax.rem(half + nsub - i, nsub) * rows_dev)
        if lean:
            arrive(f, c)
        multiply(f, c)
        if c == chunks - 1:
            for i in range(1, nquad):
                part_copy(f, i).start()

    def total(f, h):
        start = pl.multiple_of(quad * share, 8)
        value = acc[f, pl.ds(start, share), :] if h == 0 else parts[f, h]
        for i in range(h + nsub, nquad, nsub):
            value = value + parts[f, i]
        return value

    for i in range(1, nquad):
        part_copy(0, i).wait_recv()
    for i in range(1, nquad):
        part_copy(1, i).wait_recv()
    product = total(0, 0) * total(1, 0)
    for h in range(1, nsub):
        product = product + total(0, h) * total(1, h)
    result = live * lax.dot_general(
        product,
        mapping,
        (((1,), (0,)), ((), ())),
        precision=lax.Precision.HIGHEST,
        preferred_element_type=jnp.float32,
    )
    out_ref[...] = result.T[: out_ref.shape[0], :]

    for f in range(2):
        for c in range(chunks):
            fac_all(f, c).wait_send()
        for i in range(1, nquad):
            part_copy(f, i).wait_send()
    if lean:
        for f, c in pieces:
            for way, ends in ((0, last), (1, first)):

                @pl.when(jnp.logical_not(ends))
                def _():
                    relay_copy(f, c, way).wait_send()


def on_device(
    activation,
    cotangent,
    query_output_factor,
    query_input_factor,
    query_dest,
    query_cluster,
    token_cluster,
    token_count,
):
    ntok = lax.axis_size("tok")
    nsub = lax.axis_size("sub")
    nwide = lax.axis_size("width")
    local_q, topc = query_dest.shape
    rows_dev, depth = activation.shape
    rank = query_output_factor.shape[1]
    block_rows = rows_dev * nsub
    nquad = nwide * nsub
    share = block_rows // nquad
    lanes = -(-ntok * local_q // 128) * 128
    lines = -(-2 * topc // 8) * 8
    ngroup = lax.axis_size("groups")
    chunks = CHUNKS
    dma = pltpu.SemaphoreType.DMA
    vmem = pl.BlockSpec(memory_space=pltpu.VMEM)
    smem = pl.BlockSpec(memory_space=pltpu.SMEM)
    hbm = pl.BlockSpec(memory_space=pl.ANY)
    dest, clus = query_dest.T, query_cluster.T
    lists, count = pl.pallas_call(
        functools.partial(meta_kernel, ngroup, ntok),
        out_shape=(
            jax.ShapeDtypeStruct((lines, lanes), jnp.int32),
            jax.ShapeDtypeStruct((1,), jnp.int32),
        ),
        in_specs=[smem, smem],
        out_specs=(vmem, smem),
        scratch_shapes=[
            pltpu.VMEM((lines, lanes), jnp.int32),
            pltpu.VMEM((ngroup * ntok, lines, lanes), jnp.int32),
            dma((ngroup * ntok,)),
            dma((ngroup * ntok,)),
        ],
        compiler_params=pltpu.CompilerParams(collective_id=0, has_side_effects=True),
    )(dest, clus)

    def call(lean, *args):
        seats = 1 if lean else CAP
        places = ntok + 4 if lean else ntok
        width = places * seats * rank
        return pl.pallas_call(
            functools.partial(kernel, ntok, nwide, nsub, chunks, lean),
            out_shape=jax.ShapeDtypeStruct((ntok * local_q, share), jnp.float32),
            in_specs=[hbm, hbm, vmem, vmem, smem, vmem, vmem, smem],
            out_specs=vmem,
            scratch_shapes=[
                pltpu.VMEM((2, block_rows, depth), jnp.float32),
                pltpu.VMEM((2, block_rows, depth), jnp.bfloat16),
                pltpu.VMEM((2, block_rows, depth), jnp.bfloat16),
                pltpu.VMEM((2, ntok, seats * rank, depth), jnp.bfloat16),
                pltpu.VMEM((2, places, seats * rank, depth), jnp.bfloat16),
                pltpu.VMEM((2, block_rows, width), jnp.float32),
                pltpu.VMEM((2, nquad, share, width), jnp.float32),
                pltpu.VMEM((2, 2, rank, depth), jnp.bfloat16),
                dma((2,)),
                dma((2, nsub)),
                dma((2, nsub)),
                dma((2, 2, chunks)),
                dma((2, 2, chunks)),
                dma((2, chunks)),
                dma((2, chunks)),
                dma((2, nquad)),
                dma((2, nquad)),
            ],
            compiler_params=pltpu.CompilerParams(
                collective_id=1 if lean else 2,
                has_side_effects=True,
                vmem_limit_bytes=56 * 2**20,
            ),
        )(*args)

    scores = lax.cond(
        count[0] <= 1,
        functools.partial(call, True),
        functools.partial(call, False),
        activation,
        cotangent,
        query_output_factor,
        query_input_factor,
        dest,
        lists,
        token_cluster,
        token_count,
    )
    return scores.T


def solution(mesh):
    placed = (
        P(("groups", "tok", "sub"), "width"),
        P(("groups", "tok", "sub"), "width"),
        P(("groups", "tok"), "sub", "width"),
        P(("groups", "tok"), "sub", "width"),
        P(("groups", "tok"), None),
        P(("groups", "tok"), None),
        P(("groups", "tok")),
        P("groups"),
    )
    return jax.shard_map(
        on_device,
        mesh=mesh,
        in_specs=placed,
        out_specs=P(("groups", "tok", "width", "sub"), None),
        check_vma=False,
    )
```
